32 devices in a mesh: section: 2 (over core), shard: 4 (over z), rep: 4 (over y, x).
Axes of the slice: x: 2, y: 2, z: 4, core: 2. Of those that a mesh axis runs over, the one named last changes fastest.
Arguments:
- images: bfloat16 [4, 32, 196, 512], P(None, ('shard', 'rep')), may hold values from -6 to 6
- cotangent: bfloat16 [4, 32, 196, 512], P(None, ('shard', 'rep')), may hold values from -6 to 6
- region: int32 [196], replicated, may hold values from 0 to 3
- rel_index: int32 [49, 49], replicated, may hold values from 0 to 168
- norm1_gain: float32 [2, 512], P('section'), may hold values from 0.5 to 1.5
- norm1_bias: float32 [2, 512], P('section'), may hold values from -1.25 to 1.25
- w_qkv: bfloat16 [2, 512, 1536], P('section', 'shard'), may hold values from -0.25 to 0.25
- qv_bias: float32 [2, 1024], P('section'), may hold values from -1.25 to 1.25
- rel_table: float32 [2, 169, 16], P('section'), may hold values from -6 to 6
- w_proj: bfloat16 [2, 512, 512], P('section', 'shard'), may hold values from -0.75 to 0.75
- proj_bias: float32 [2, 512], P('section'), may hold values from -1.25 to 1.25
- norm2_gain: float32 [2, 512], P('section'), may hold values from 0.5 to 1.5
- norm2_bias: float32 [2, 512], P('section'), may hold values from -1.25 to 1.25
- w_fc1: bfloat16 [2, 512, 2048], P('section', 'shard'), may hold values from -0.25 to 0.25
- fc1_bias: float32 [2, 2048], P('section'), may hold values from -1.25 to 1.25
- w_fc2: bfloat16 [2, 2048, 512], P('section', 'shard'), may hold values from -0.125 to 0.125
- fc2_bias: float32 [2, 512], P('section'), may hold values from -1.25 to 1.25
Outputs:
- section_out: bfloat16 [2, 4, 32, 196, 512], P('section', None, ('shard', 'rep'))
- input_grad: float32 [2, 4, 32, 196, 512], P('section', None, ('shard', 'rep'))
- grad_norm1_gain: float32 [2, 512], P('section')
- grad_norm1_bias: float32 [2, 512], P('section')
- grad_qkv: float32 [2, 512, 1536], P('section', 'shard')
- grad_qv_bias: float32 [2, 1024], P('section')
- grad_table: float32 [2, 169, 16], P('section')
- grad_proj: float32 [2, 512, 512], P('section', 'shard')
- grad_proj_bias: float32 [2, 512], P('section')
- grad_norm2_gain: float32 [2, 512], P('section')
- grad_norm2_bias: float32 [2, 512], P('section')
- grad_fc1: float32 [2, 512, 2048], P('section', 'shard')
- grad_fc1_bias: float32 [2, 2048], P('section')
- grad_fc2: float32 [2, 2048, 512], P('section', 'shard')
- grad_fc2_bias: float32 [2, 512], P('section')
The draws below stay inside these ranges and needn't reach their ends.
All inputs are finite; a program needn't handle non-finite values.
Results may differ from the reference program's by a relative error of at most 0.023.
Values may be sent and summed in bfloat16 or wider, within the bound.
A program may use at most 256 MiB of HBM per device.

```python
import math
import jax
import jax.numpy as jnp
from jax import lax

C = 512
HEADS = 16
HEAD = 32
FF = 2048
WIN = 7
GRID = 14
SHIFT = 3
REGIONS = 4
MICRO = 4
IMG = 2
TABLE = 169
IMAGES = 32
N_REP = 4


def with_ends(result, own_key, low, top_value):
    dims = result.shape
    place = [jax.random.randint(jax.random.fold_in(own_key, axis), (), 0, dims[axis]) for axis in range(len(dims))]
    result = result.at[tuple(place)].set(low)
    longest = dims.index(max(dims))
    place[longest] = (place[longest] + 1) % dims[longest]
    return result.at[tuple(place)].set(top_value)


def block_levels(own_key, shape, cuts, smallest, largest):
    factor_of = 1.0
    for axis_at, parts in cuts:
        steps = jax.random.uniform(jax.random.fold_in(jax.random.fold_in(own_key, 6), axis_at), (parts,), jnp.float32, smallest / len(cuts), largest / len(cuts))
        factor_of = factor_of * jnp.repeat(jnp.exp(steps), shape[axis_at] // parts).reshape((-1,) + (1,) * (len(shape) - 1 - axis_at))
    return factor_of


def bell_draw(rng, dims, spread, limit, pieces=(), held_as=jnp.bfloat16):
    values = jax.random.normal(rng, dims, jnp.float32) * spread
    if len(pieces) > 0:
        values = block_levels(rng, dims, pieces, -0.22, 0.18) * values
    return jnp.clip(values, min=-limit, max=limit).astype(held_as)


def setup_inputs(seed: int = 0) -> dict:
    seeds = jax.random.split(jax.random.key(seed), 18)
    return {
        "images": bell_draw(seeds[0], (MICRO, IMAGES, GRID * GRID, C), 1.0, 6.0, ((1, 16),)),
        "cotangent": bell_draw(seeds[1], (MICRO, IMAGES, GRID * GRID, C), 1.0, 6.0, ((1, 16),)),
        "region": with_ends(jax.random.randint(seeds[2], (GRID * GRID,), 0, REGIONS), jax.random.fold_in(seeds[2], 1), 0, REGIONS - 1).astype(jnp.int32),
        "rel_index": with_ends(jax.random.randint(seeds[3], (WIN * WIN, WIN * WIN), 0, TABLE), jax.random.fold_in(seeds[3], 1), 0, TABLE - 1).astype(jnp.int32),
        "norm1_gain": jnp.clip(1.0 + 0.1 * jax.random.normal(seeds[4], (2, C), jnp.float32), 0.5, 1.5),
        "norm1_bias": bell_draw(seeds[5], (2, C), 0.2, 1.25, ((0, 2),), jnp.float32),
        "w_qkv": bell_draw(seeds[6], (2, C, 3 * C), C ** -0.5, 0.25, ((0, 2), (1, 4))),
        "qv_bias": bell_draw(seeds[7], (2, 2 * C), 0.2, 1.25, ((0, 2),), jnp.float32),
        "rel_table": bell_draw(seeds[8], (2, TABLE, HEADS), 1.0, 6.0, ((0, 2),), jnp.float32),
        "w_proj": bell_draw(seeds[9], (2, C, C), (C // 8) ** -0.5, 0.75, ((0, 2), (1, 4))),
        "proj_bias": bell_draw(seeds[10], (2, C), 0.2, 1.25, ((0, 2),), jnp.float32),
        "norm2_gain": jnp.clip(1.0 + 0.1 * jax.random.normal(seeds[11], (2, C), jnp.float32), 0.5, 1.5),
        "norm2_bias": bell_draw(seeds[12], (2, C), 0.2, 1.25, ((0, 2),), jnp.float32),
        "w_fc1": bell_draw(seeds[13], (2, C, FF), C ** -0.5, 0.25, ((0, 2), (1, 4))),
        "fc1_bias": bell_draw(seeds[14], (2, FF), 0.2, 1.25, ((0, 2),), jnp.float32),
        "w_fc2": bell_draw(seeds[15], (2, FF, C), FF ** -0.5, 0.125, ((0, 2), (1, 4))),
        "fc2_bias": bell_draw(seeds[16], (2, C), 0.2, 1.25, ((0, 2),), jnp.float32),
    }


HIGH = lax.Precision.HIGHEST

@jax.custom_vjp
def low(v):
    return lax.optimization_barrier(v.astype(jnp.bfloat16)).astype(jnp.float32)

@jax.custom_vjp
def low_back(v):
    return v

def low_keep(v):
    return (low(v), None)

def low_pass(kept, grad):
    return (grad,)

def back_keep(v):
    return (v, None)

def back_low(kept, grad):
    return (low(grad),)
low.defvjp(low_keep, low_pass)
low_back.defvjp(back_keep, back_low)

def layer_norm(values, gain, beta_term):
    average = lax.optimization_barrier(jnp.mean(values, -1, keepdims=True))
    centred = values - average
    variance = lax.optimization_barrier(jnp.mean(centred * centred, -1, keepdims=True))
    return centred * lax.rsqrt(variance + 1e-05) * gain + beta_term

def to_windows(tensor, offset):
    images_here, tokens_here, channels = tensor.shape
    per_side = GRID // WIN
    lattice = tensor.reshape(images_here, GRID, GRID, channels)
    lattice = jnp.roll(lattice, (-offset, -offset), (1, 2))
    lattice = lattice.reshape(images_here, per_side, WIN, per_side, WIN, channels).transpose(0, 1, 3, 2, 4, 5)
    return lattice.reshape(images_here * per_side * per_side, WIN * WIN, channels)

def from_windows(tensor, offset, images_here):
    channels = tensor.shape[-1]
    per_side = GRID // WIN
    lattice = tensor.reshape(images_here, per_side, per_side, WIN, WIN, channels).transpose(0, 1, 3, 2, 4, 5)
    lattice = lattice.reshape(images_here, GRID, GRID, channels)
    lattice = jnp.roll(lattice, (offset, offset), (1, 2))
    return lattice.reshape(images_here, GRID * GRID, channels)

def swin_layer(inputs, params, offset, masked, onehot, region):
    norm1_gain, norm1_bias, w_qkv, qv_bias, rel_table, w_proj, proj_bias, norm2_gain, norm2_bias, w_fc1, fc1_bias, w_fc2, fc2_bias = params
    images_here = inputs.shape[0]
    channels = inputs.shape[-1]
    heads_all = channels // HEAD
    scale_qk = 1.0 / math.sqrt(HEAD)
    normed = low(layer_norm(inputs, norm1_gain, norm1_bias))
    full_bias = jnp.concatenate([qv_bias[:channels], jnp.zeros((channels,), jnp.float32), qv_bias[channels:]])
    projected = jnp.einsum('bnc,ce->bne', normed, w_qkv, precision=HIGH) + full_bias
    queries = low_back(low(projected[..., :channels]))
    keys_all = low_back(low(projected[..., channels:2 * channels]))
    values_all = low_back(low(projected[..., 2 * channels:]))

    def split_heads(tensor):
        windowed = to_windows(tensor, offset)
        return windowed.reshape(windowed.shape[0], WIN * WIN, heads_all, HEAD)
    win_q = split_heads(queries)
    win_k = split_heads(keys_all)
    win_v = split_heads(values_all)
    rel_bias = jnp.einsum('ijr,rh->hij', onehot, rel_table, precision=HIGH)
    scores = jnp.einsum('wihd,wjhd->whij', win_q, win_k, precision=HIGH) * scale_qk + rel_bias[None]
    if masked:
        labels = to_windows(region.reshape(1, -1, 1), 0)[..., 0]
        mask_add = jnp.where(labels[:, :, None] == labels[:, None, :], 0.0, -100.0).astype(jnp.float32)
        per_image = mask_add.shape[0]
        scores = (scores.reshape(images_here, per_image, heads_all, WIN * WIN, WIN * WIN) + mask_add[None, :, None]).reshape(scores.shape)
    scores = low_back(scores)
    weights = low(jax.nn.softmax(scores, axis=-1))
    attended = low_back(low(jnp.einsum('whij,wjhd->wihd', weights, win_v, precision=HIGH)))
    merged = from_windows(attended.reshape(attended.shape[0], WIN * WIN, channels), offset, images_here)
    branch = low_back(jnp.einsum('bnc,ce->bne', merged, w_proj, precision=HIGH) + proj_bias)
    middle = inputs + branch
    normed_two = low(layer_norm(middle, norm2_gain, norm2_bias))
    hidden = low_back(jnp.einsum('bnc,cf->bnf', normed_two, w_fc1, precision=HIGH) + fc1_bias)
    activated = low(jax.nn.gelu(hidden, approximate=False))
    branch_two = low_back(jnp.einsum('bnf,fc->bnc', activated, w_fc2, precision=HIGH) + fc2_bias)
    return middle + branch_two

def reference(images, cotangent, region, rel_index, norm1_gain, norm1_bias, w_qkv, qv_bias, rel_table, w_proj, proj_bias, norm2_gain, norm2_bias, w_fc1, fc1_bias, w_fc2, fc2_bias):
    every = (norm1_gain, norm1_bias, w_qkv, qv_bias, rel_table, w_proj, proj_bias, norm2_gain, norm2_bias, w_fc1, fc1_bias, w_fc2, fc2_bias)
    onehot = (rel_index[:, :, None] == jnp.arange(TABLE, dtype=jnp.int32)[None, None, :]).astype(jnp.float32)
    params_first = tuple((item[0].astype(jnp.float32) for item in every))
    params_second = tuple((item[1].astype(jnp.float32) for item in every))
    group = IMG * N_REP
    blocks = MICRO * IMAGES // group
    inputs_all = images.astype(jnp.float32).reshape(blocks, group, GRID * GRID, C)
    cot_all = cotangent.astype(jnp.float32).reshape(blocks, group, GRID * GRID, C)

    def first_layer(inputs, *params):
        return swin_layer(inputs, params, 0, False, onehot, region)

    def second_layer(inputs, *params):
        return swin_layer(inputs, params, SHIFT, True, onehot, region)

    def one_block(totals, pair):
        inputs, cot_block = pair
        hidden_out, back_first = jax.vjp(first_layer, inputs, *params_first)
        sent = low(hidden_out)
        final_out, back_second = jax.vjp(second_layer, sent, *params_second)
        grads_second = back_second(cot_block)
        grad_hidden = grads_second[0]
        grads_first = back_first(low(grad_hidden))
        totals = (jax.tree.map(jnp.add, totals[0], tuple(grads_first[1:])), jax.tree.map(jnp.add, totals[1], tuple(grads_second[1:])))
        return (totals, (sent, low(final_out), grads_first[0], grad_hidden))
    zeros = (tuple((jnp.zeros_like(item) for item in params_first)), tuple((jnp.zeros_like(item) for item in params_second)))
    totals, (sent_all, final_all, grad_x_all, grad_h_all) = lax.scan(one_block, zeros, (inputs_all, cot_all))
    shape_out = (2, MICRO, IMAGES, GRID * GRID, C)
    section_out = jnp.stack([sent_all, final_all]).reshape(shape_out).astype(jnp.bfloat16)
    input_grad = jnp.stack([grad_x_all, grad_h_all]).reshape(shape_out)
    stacked = [jnp.stack([totals[0][which], totals[1][which]]) for which in range(13)]
    return (section_out, input_grad, stacked[0], stacked[1], stacked[2], stacked[3], stacked[4], stacked[5], stacked[6], stacked[7], stacked[8], stacked[9], stacked[10], stacked[11], stacked[12])
```

```python
import functools
import math

import jax
import jax.numpy as jnp
import numpy as np
from jax import lax
from jax.experimental import pallas as pl
from jax.experimental.pallas import tpu as pltpu
from jax.sharding import PartitionSpec as P

HEAD = 32
WIN = 7
GRID = 14
SHIFT = 3
ROWS = 256
SLOT = 64
PAIR = 128
CHUNK = 512
FAR = -1e30
SCALE = 1.0 / math.sqrt(HEAD)


def mm(left, right):
    return jnp.dot(left, right, preferred_element_type=jnp.float32)


def mm_t(left, right):
    return lax.dot_general(
        left, right, (((1,), (1,)), ((), ())), preferred_element_type=jnp.float32
    )


def mm_outer(left, right):
    return lax.dot_general(
        left, right, (((0,), (0,)), ((), ())), preferred_element_type=jnp.float32
    )


def unit(values):
    centred = values - jnp.mean(values, -1, keepdims=True)
    inverse = lax.rsqrt(jnp.mean(centred * centred, -1, keepdims=True) + 1e-05)
    return centred * inverse, inverse


def unit_back(grad, unit_rows, inverse, gain):
    scaled = grad * gain
    return inverse * (
        scaled
        - jnp.mean(scaled, -1, keepdims=True)
        - unit_rows * jnp.mean(scaled * unit_rows, -1, keepdims=True)
    )


def col(values):
    return jnp.sum(values, axis=0, keepdims=True)


def layer_kernel(backward, *refs):
    if backward:
        (x_ref, cot_ref, perm, back, wqkv, bqkv, wproj, vecs, w1, b1, w2, bias, hm,
         out_ref, dx_ref, gqkv_o, gproj_o, g1_o, g2_o, gvec, gcol, gfc1b, drel,
         x_s, a_s, qkv_s, att_s, b_s, acc_s, probs_s, u1_s, u2_s,
         dy_s, db_s, dqkv_s, datt_s, gqkv, gproj, g1, g2) = refs
        for ref in (gvec, gcol, gfc1b, drel, gqkv, gproj, g1, g2):
            ref[...] = jnp.zeros_like(ref)
    else:
        (x_ref, perm, back, wqkv, bqkv, wproj, vecs, w1, b1, w2, bias, hm, out_ref,
         x_s, a_s, qkv_s, att_s, b_s, acc_s) = refs
    channels = wproj.shape[0]
    groups = channels // PAIR
    steps = (ROWS // PAIR) * groups
    heads = PAIR // HEAD

    def place(t):
        rows = pl.ds(pl.multiple_of((t // groups) * PAIR, PAIR), PAIR)
        g = t % groups

        def lanes(which):
            return pl.ds(pl.multiple_of(which * channels + g * PAIR, PAIR), PAIR)

        return rows, g, lanes

    def spread(block):
        return jnp.concatenate([block] * heads, axis=0) * hm[...]

    def gathered(stack):
        total = stack[:PAIR] * hm[:PAIR].astype(jnp.float32)
        for h in range(1, heads):
            part = slice(h * PAIR, (h + 1) * PAIR)
            total = total + stack[part] * hm[part].astype(jnp.float32)
        return total

    def one_image(i, carry):
        x = mm(perm[...], x_ref[i])
        x_s[...] = x
        unit_one, inv_one = unit(x)
        a_s[...] = (unit_one * vecs[0:1] + vecs[1:2]).astype(jnp.bfloat16)
        if backward:
            u1_s[...] = unit_one
        for part in range(3):
            cols = slice(part * channels, (part + 1) * channels)
            qkv_s[:, cols] = (mm(a_s[...], wqkv[:, cols]) + bqkv[:, cols]).astype(jnp.bfloat16)

        def attend(t, c):
            rows, g, lanes = place(t)
            scores = mm_t(qkv_s[rows, lanes(0)], spread(qkv_s[rows, lanes(1)]))
            scores = scores * SCALE + bias[t]
            parts = []
            for h in range(heads):
                s = scores[:, h * PAIR:(h + 1) * PAIR]
                e = jnp.exp(s - jnp.max(s, -1, keepdims=True))
                parts.append(e * (1.0 / jnp.sum(e, -1, keepdims=True)))
            probs = jnp.concatenate(parts, axis=1)
            if backward:
                probs_s[t] = probs
            att_s[rows, lanes(0)] = mm(
                probs.astype(jnp.bfloat16), spread(qkv_s[rows, lanes(2)])
            ).astype(jnp.bfloat16)
            return c

        lax.fori_loop(0, steps, attend, 0)
        middle = x_s[...] + (mm(att_s[...], wproj[...]) + vecs[2:3])
        x_s[...] = middle
        unit_two, inv_two = unit(middle)
        b_s[...] = (unit_two * vecs[3:4] + vecs[4:5]).astype(jnp.bfloat16)
        acc_s[...] = jnp.zeros_like(acc_s)
        if backward:
            u2_s[...] = unit_two
            dy_s[...] = mm(perm[...], cot_ref[i]).astype(jnp.bfloat16)
            db_s[...] = jnp.zeros_like(db_s)

        def ffn(c, k):
            cols = pl.ds(pl.multiple_of(c * CHUNK, CHUNK), CHUNK)
            hidden = mm(b_s[...], w1[:, cols]) + b1[:, cols]
            cdf = 0.5 * (1.0 + lax.erf(hidden * (1.0 / math.sqrt(2.0))))
            act = (hidden * cdf).astype(jnp.bfloat16)
            acc_s[...] += mm(act, w2[cols, :])
            if backward:
                pdf = jnp.exp(-0.5 * hidden * hidden) * (1.0 / math.sqrt(2.0 * math.pi))
                dact = mm_t(dy_s[...], w2[cols, :])
                dhid_f = dact * (cdf + hidden * pdf)
                dhid = dhid_f.astype(jnp.bfloat16)
                g2[cols, :] += mm_outer(act, dy_s[...])
                g1[:, cols] += mm_outer(b_s[...], dhid)
                gfc1b[:, cols] += col(dhid.astype(jnp.float32))
                db_s[...] += mm_t(dhid, w1[:, cols])
            return k

        lax.fori_loop(0, w1.shape[1] // CHUNK, ffn, 0)
        out = (x_s[...] + (acc_s[...] + vecs[5:6])).astype(jnp.bfloat16)
        out_ref[i] = mm(back[...], out).astype(jnp.bfloat16)
        if not backward:
            return carry
        db = db_s[...]
        gvec[3:4] += col(db * u2_s[...])
        gvec[4:5] += col(db)
        dy = dy_s[...].astype(jnp.float32)
        gvec[5:6] += col(dy)
        dmid = dy + unit_back(db, u2_s[...], inv_two, vecs[3:4])
        x_s[...] = dmid
        dz = dmid.astype(jnp.bfloat16)
        gvec[2:3] += col(dz.astype(jnp.float32))
        gproj[...] += mm_outer(att_s[...], dz)
        datt_s[...] = mm_t(dz, wproj[...]).astype(jnp.bfloat16)

        def attend_back(t, c):
            rows, g, lanes = place(t)
            datt = datt_s[rows, lanes(0)]
            probs = probs_s[t]
            dprobs = mm_t(datt, spread(qkv_s[rows, lanes(2)]))
            dqkv_s[rows, lanes(2)] = gathered(
                mm_outer(probs.astype(jnp.bfloat16), datt)
            ).astype(jnp.bfloat16)
            parts = []
            for h in range(heads):
                here = slice(h * PAIR, (h + 1) * PAIR)
                p = probs[:, here]
                d = dprobs[:, here]
                parts.append(p * (d - jnp.sum(p * d, -1, keepdims=True)))
            dscores = jnp.concatenate(parts, axis=1).astype(jnp.bfloat16)
            drel[g] += dscores.astype(jnp.float32)
            dqkv_s[rows, lanes(0)] = (
                mm(dscores, spread(qkv_s[rows, lanes(1)])) * SCALE
            ).astype(jnp.bfloat16)
            dqkv_s[rows, lanes(1)] = (
                gathered(mm_outer(dscores, qkv_s[rows, lanes(0)])) * SCALE
            ).astype(jnp.bfloat16)
            return c

        lax.fori_loop(0, steps, attend_back, 0)
        for part in range(3):
            cols = slice(part * channels, (part + 1) * channels)
            gqkv[:, cols] += mm_outer(a_s[...], dqkv_s[:, cols])
            gcol[:, cols] += col(dqkv_s[:, cols].astype(jnp.float32))
        da = mm_t(dqkv_s[...], wqkv[...])
        gvec[0:1] += col(da * u1_s[...])
        gvec[1:2] += col(da)
        dx = x_s[...] + unit_back(da, u1_s[...], inv_one, vecs[0:1])
        high = dx.astype(jnp.bfloat16)
        rest = (dx - high.astype(jnp.float32)).astype(jnp.bfloat16)
        dx_ref[i] = mm(back[...], high) + mm(back[...], rest)
        return carry

    lax.fori_loop(0, x_ref.shape[0], one_image, 0)
    if backward:
        gqkv_o[...] = gqkv[...].astype(jnp.bfloat16)
        gproj_o[...] = gproj[...].astype(jnp.bfloat16)
        g1_o[...] = g1[...].astype(jnp.bfloat16)
        g2_o[...] = g2[...].astype(jnp.bfloat16)


def call_layer(x, cot, consts, mats, small):
    perm, back, hm = consts
    wqkv, wproj, w1, w2 = mats
    bqkv, vecs, b1, bias = small
    backward = cot is not None
    n = x.shape[0]
    c, f = w1.shape
    low, full = jnp.bfloat16, jnp.float32
    t = bias.shape[0]
    tokens = (ROWS, c)
    heads = PAIR // HEAD
    outs = [jax.ShapeDtypeStruct((n,) + tokens, low)]
    scratch = [
        pltpu.VMEM(tokens, full),
        pltpu.VMEM(tokens, low),
        pltpu.VMEM((ROWS, 3 * c), low),
        pltpu.VMEM(tokens, low),
        pltpu.VMEM(tokens, low),
        pltpu.VMEM(tokens, full),
    ]
    if backward:
        outs += [
            jax.ShapeDtypeStruct((n,) + tokens, full),
            jax.ShapeDtypeStruct(wqkv.shape, low),
            jax.ShapeDtypeStruct(wproj.shape, low),
            jax.ShapeDtypeStruct(w1.shape, low),
            jax.ShapeDtypeStruct(w2.shape, low),
            jax.ShapeDtypeStruct((8, c), full),
            jax.ShapeDtypeStruct((1, 3 * c), full),
            jax.ShapeDtypeStruct((1, f), full),
            jax.ShapeDtypeStruct((c // PAIR, PAIR, heads * PAIR), full),
        ]
        scratch += [
            pltpu.VMEM((t, PAIR, heads * PAIR), full),
            pltpu.VMEM(tokens, full),
            pltpu.VMEM(tokens, full),
            pltpu.VMEM(tokens, low),
            pltpu.VMEM(tokens, full),
            pltpu.VMEM((ROWS, 3 * c), low),
            pltpu.VMEM(tokens, low),
            pltpu.VMEM(wqkv.shape, full),
            pltpu.VMEM(wproj.shape, full),
            pltpu.VMEM(w1.shape, full),
            pltpu.VMEM(w2.shape, full),
        ]
    args = (x,) + ((cot,) if backward else ())
    args += (perm, back, wqkv, bqkv, wproj, vecs, w1, b1, w2, bias, hm)
    vmem = pl.BlockSpec(memory_space=pltpu.VMEM)
    return pl.pallas_call(
        functools.partial(layer_kernel, backward),
        out_shape=outs,
        in_specs=[vmem] * len(args),
        out_specs=[vmem] * len(outs),
        scratch_shapes=scratch,
        compiler_params=pltpu.CompilerParams(vmem_limit_bytes=58 * 2**20),
        cost_estimate=pl.CostEstimate(
            flops=2 * n * ROWS * c * (4 * c + 2 * f) * (3 if backward else 1),
            bytes_accessed=2 * c * (4 * c + 2 * f),
            transcendentals=n * ROWS * f,
        ),
    )(*args)


def window_order(offset):
    matrix = np.zeros((ROWS, ROWS), np.float32)
    side = GRID // WIN
    for w in range(side * side):
        for i in range(WIN * WIN):
            row = (w // side) * WIN + i // WIN
            column = (w % side) * WIN + i % WIN
            token = ((row + offset) % GRID) * GRID + (column + offset) % GRID
            matrix[w * SLOT + i, token] = 1.0
    return matrix


def window_bias(rel, mask):
    heads = rel.shape[0]
    count = mask.shape[0]
    area = WIN * WIN
    more = SLOT - area
    block = rel[None] + mask[:, None]
    block = jnp.pad(block, ((0, 0), (0, 0), (0, more), (0, 0)))
    block = jnp.pad(block, ((0, 0), (0, 0), (0, 0), (0, more)), constant_values=FAR)
    block = block.reshape(count // 2, 2, heads, SLOT, SLOT)
    first = jnp.pad(block[:, 0], ((0, 0), (0, 0), (0, 0), (0, SLOT)), constant_values=FAR)
    second = jnp.pad(block[:, 1], ((0, 0), (0, 0), (0, 0), (SLOT, 0)), constant_values=FAR)
    both = jnp.concatenate([first, second], axis=2)
    per = PAIR // HEAD
    both = both.reshape(count // 2, heads // per, per, PAIR, PAIR).transpose(0, 1, 3, 2, 4)
    return both.reshape(count // 2 * (heads // per), PAIR, per * PAIR)


def table_grad(drel, onehot):
    groups = drel.shape[0]
    area = WIN * WIN
    split = drel.reshape(groups, 2, SLOT, PAIR // HEAD, 2, SLOT)
    total = split[:, 0, :area, :, 0, :area] + split[:, 1, :area, :, 1, :area]
    return jnp.einsum("ijr,gihj->rgh", onehot, total, precision=lax.Precision.HIGHEST).reshape(
        onehot.shape[-1], -1
    )


def to_windows(tensor):
    side = GRID // WIN
    lattice = tensor.reshape(side, WIN, side, WIN).transpose(0, 2, 1, 3)
    return lattice.reshape(side * side, WIN * WIN)


def shards(
    images,
    cotangent,
    region,
    rel_index,
    norm1_gain,
    norm1_bias,
    w_qkv,
    qv_bias,
    rel_table,
    w_proj,
    proj_bias,
    norm2_gain,
    norm2_bias,
    w_fc1,
    fc1_bias,
    w_fc2,
    fc2_bias,
):
    section_id = lax.axis_index("section")
    first = section_id == 0
    micro, per, tokens, channels = images.shape
    half = micro // 2
    table_rows = rel_table.shape[1]
    heads = rel_table.shape[2]
    hidden = fc1_bias.shape[1]
    own_mats = tuple(
        lax.all_gather(part[0], "shard", axis=0, tiled=True)
        for part in (w_qkv, w_proj, w_fc1, w_fc2)
    )
    from_zero = [(0, 1)]
    from_one = [(1, 0)]

    def moved(tree, route):
        return jax.tree.map(lambda part: lax.ppermute(part, "section", route), tree)

    def choose(on_zero, on_one):
        return jax.tree.map(lambda l, r: jnp.where(first, l, r), on_zero, on_one)

    mats_zero = choose(own_mats, moved(own_mats, from_zero))
    mats_one = choose(moved(own_mats, from_one), own_mats)
    small_list = (
        norm1_gain, norm1_bias, proj_bias, norm2_gain, norm2_bias, fc2_bias, qv_bias, fc1_bias,
        rel_table,
    )
    small_flat = jnp.concatenate([part.reshape(-1) for part in small_list])
    small_both = lax.all_gather(small_flat, "section", axis=0)
    onehot = (
        rel_index[:, :, None] == jnp.arange(table_rows, dtype=jnp.int32)[None, None, :]
    ).astype(jnp.float32)
    labels = to_windows(region)
    region_mask = jnp.where(labels[:, :, None] == labels[:, None, :], 0.0, -100.0).astype(
        jnp.float32
    )

    def small_of(layer):
        flat = small_both[layer]
        six = flat[: 6 * channels].reshape(6, channels)
        vecs = jnp.pad(six, ((0, 2), (0, 0)))
        at = 6 * channels
        qv = flat[at:at + 2 * channels]
        at += 2 * channels
        b1 = flat[at:at + hidden]
        at += hidden
        table = flat[at:].reshape(table_rows, heads)
        bqkv = jnp.concatenate([qv[:channels], jnp.zeros((channels,), jnp.float32), qv[channels:]])
        rel = jnp.einsum("ijr,rh->hij", onehot, table, precision=lax.Precision.HIGHEST)
        mask = region_mask if layer == 1 else jnp.zeros_like(region_mask)
        return (bqkv[None], vecs, b1[None], window_bias(rel, mask))

    lane_head = np.arange(PAIR) // HEAD
    hm = np.zeros((PAIR // HEAD, PAIR, PAIR), np.float32)
    for h in range(PAIR // HEAD):
        hm[h] = lane_head == h
    hm = jnp.asarray(hm.reshape(-1, PAIR), jnp.bfloat16)

    def consts_of(offset):
        perm = window_order(offset)
        return jnp.asarray(perm, jnp.bfloat16), jnp.asarray(perm.T, jnp.bfloat16), hm

    def mine(array):
        part = lax.dynamic_slice_in_dim(array, section_id * half, half, 0)
        part = part.reshape(half * per, tokens, channels)
        return jnp.pad(part, ((0, 0), (0, ROWS - tokens), (0, 0)))

    def trimmed(array):
        return array[:, :tokens].reshape(half, per, tokens, channels)

    x0 = mine(images)
    cot = mine(cotangent)
    consts_zero, consts_one = consts_of(0), consts_of(SHIFT)
    small_zero, small_one = small_of(0), small_of(1)
    (x1,) = call_layer(x0, None, consts_zero, mats_zero, small_zero)
    res_one = call_layer(x1, cot, consts_one, mats_one, small_one)
    out_one, dx_one, big_one = res_one[0], res_one[1], tuple(res_one[2:6])
    sent_one = moved((trimmed(out_one), trimmed(dx_one), big_one), from_zero)
    res_zero = call_layer(x0, dx_one.astype(jnp.bfloat16), consts_zero, mats_zero, small_zero)
    dx_zero, big_zero = res_zero[1], tuple(res_zero[2:6])
    x1_there = moved(trimmed(x1), from_one)
    dx_there, big_there = moved((trimmed(dx_zero), big_zero), from_one)

    def whole(zero_own, zero_there, one_own, one_there):
        on_zero = jnp.concatenate([zero_own, zero_there], 0)
        on_one = jnp.concatenate([one_there, one_own], 0)
        return jnp.where(first, on_zero, on_one)[None]

    section_out = whole(trimmed(x1), x1_there, trimmed(out_one), sent_one[0])
    input_grad = whole(trimmed(dx_zero), dx_there, trimmed(dx_one), sent_one[1])

    def summed(zero_own, zero_there, one_own, one_there):
        own = jnp.where(first, zero_own, one_own).astype(jnp.float32)
        there = jnp.where(first, zero_there, one_there).astype(jnp.float32)
        return (own + there).astype(jnp.bfloat16)

    big_total = jax.tree.map(summed, big_zero, big_there, big_one, sent_one[2])
    owned = lax.psum_scatter(big_total, "shard", scatter_dimension=0, tiled=True)
    rows_qkv, rows_proj, rows_fc1, rows_fc2 = jax.tree.map(
        lambda part: part.astype(jnp.float32), lax.psum(owned, "rep")
    )

    def small_grads(res):
        gvec, gcol, gfc1b, drel = res[6:10]
        return jnp.concatenate(
            [
                gvec[:6].reshape(-1), gcol[0, :channels], gcol[0, 2 * channels:], gfc1b[0],
                table_grad(drel, onehot).reshape(-1),
            ]
        )

    small_sum = lax.psum(
        jnp.stack([small_grads(res_zero), small_grads(res_one)]), ("section", "shard", "rep")
    )
    flat = jnp.where(first, small_sum[0], small_sum[1])
    six = flat[: 6 * channels].reshape(6, 1, channels)
    at = 6 * channels
    qv_sum = flat[at:at + 2 * channels][None]
    at += 2 * channels
    fc1_sum = flat[at:at + hidden][None]
    table_sum = flat[at + hidden:].reshape(1, table_rows, heads)
    return (
        section_out,
        input_grad,
        six[0],
        six[1],
        rows_qkv[None],
        qv_sum,
        table_sum,
        rows_proj[None],
        six[2],
        six[3],
        six[4],
        rows_fc1[None],
        fc1_sum,
        rows_fc2[None],
        six[5],
    )


def solution(mesh):
    placed = (
        P(None, ("shard", "rep"), None, None),
        P(None, ("shard", "rep"), None, None),
        P(),
        P(),
        P("section", None),
        P("section", None),
        P("section", "shard", None),
        P("section", None),
        P("section", None, None),
        P("section", "shard", None),
        P("section", None),
        P("section", None),
        P("section", None),
        P("section", "shard", None),
        P("section", None),
        P("section", "shard", None),
        P("section", None),
    )
    return jax.shard_map(
        shards,
        mesh=mesh,
        in_specs=placed,
        out_specs=(
            P("section", None, ("shard", "rep"), None, None),
            P("section", None, ("shard", "rep"), None, None),
            P("section", None),
            P("section", None),
            P("section", "shard", None),
            P("section", None),
            P("section", None, None),
            P("section", "shard", None),
            P("section", None),
            P("section", None),
            P("section", None),
            P("section", "shard", None),
            P("section", None),
            P("section", "shard", None),
            P("section", None),
        ),
        check_vma=False,
    )
```

```python
import functools
import math

import jax
import jax.numpy as jnp
import numpy as np
from jax import lax
from jax.experimental import pallas as pl
from jax.experimental.pallas import tpu as pltpu
from jax.sharding import PartitionSpec as P

HEAD = 32
WIN = 7
GRID = 14
SHIFT = 3
ROWS = 256
SLOT = 64
PAIR = 128
CHUNK = 512
FAR = -1e30
SCALE = 1.0 / math.sqrt(HEAD)


def mm(left, right):
    return jnp.dot(left, right, preferred_element_type=jnp.float32)


def mm_t(left, right):
    return lax.dot_general(
        left, right, (((1,), (1,)), ((), ())), preferred_element_type=jnp.float32
    )


def mm_outer(left, right):
    return lax.dot_general(
        left, right, (((0,), (0,)), ((), ())), preferred_element_type=jnp.float32
    )


def unit(values):
    centred = values - jnp.mean(values, -1, keepdims=True)
    inverse = lax.rsqrt(jnp.mean(centred * centred, -1, keepdims=True) + 1e-05)
    return centred * inverse, inverse


def unit_back(grad, unit_rows, inverse, gain):
    scaled = grad * gain
    return inverse * (
        scaled
        - jnp.mean(scaled, -1, keepdims=True)
        - unit_rows * jnp.mean(scaled * unit_rows, -1, keepdims=True)
    )


def col(values):
    return jnp.sum(values, axis=0, keepdims=True)


def layer_kernel(backward, *refs):
    if backward:
        (x_ref, cot_ref, perm, back, wqkv, bqkv, wproj, vecs, w1, b1, w2, bias, hm,
         out_ref, dx_ref, gqkv_o, gproj_o, g1_o, g2_o, gvec, gcol, gfc1b, drel,
         x_s, a_s, qkv_s, att_s, b_s, acc_s, probs_s, u1_s, u2_s,
         dy_s, db_s, dqkv_s, datt_s, gqkv, gproj, g1, g2) = refs
        for ref in (gvec, gcol, gfc1b, drel, gqkv, gproj, g1, g2):
            ref[...] = jnp.zeros_like(ref)
    else:
        (x_ref, perm, back, wqkv, bqkv, wproj, vecs, w1, b1, w2, bias, hm, out_ref,
         x_s, a_s, qkv_s, att_s, b_s, acc_s) = refs
    channels = wproj.shape[0]
    groups = channels // PAIR
    steps = (ROWS // PAIR) * groups
    heads = PAIR // HEAD

    def place(t):
        rows = pl.ds(pl.multiple_of((t // groups) * PAIR, PAIR), PAIR)
        g = t % groups

        def lanes(which):
            return pl.ds(pl.multiple_of(which * channels + g * PAIR, PAIR), PAIR)

        return rows, g, lanes

    def spread(block):
        return jnp.concatenate([block] * heads, axis=0) * hm[...]

    def gathered(stack):
        total = stack[:PAIR] * hm[:PAIR].astype(jnp.float32)
        for h in range(1, heads):
            part = slice(h * PAIR, (h + 1) * PAIR)
            total = total + stack[part] * hm[part].astype(jnp.float32)
        return total

    def one_image(i, carry):
        x = mm(perm[...], x_ref[i])
        x_s[...] = x
        unit_one, inv_one = unit(x)
        a_s[...] = (unit_one * vecs[0:1] + vecs[1:2]).astype(jnp.bfloat16)
        if backward:
            u1_s[...] = unit_one
        for part in range(3):
            cols = slice(part * channels, (part + 1) * channels)
            qkv_s[:, cols] = (mm(a_s[...], wqkv[:, cols]) + bqkv[:, cols]).astype(jnp.bfloat16)

        def attend(t, c):
            rows, g, lanes = place(t)
            scores = mm_t(qkv_s[rows, lanes(0)], spread(qkv_s[rows, lanes(1)]))
            scores = scores * SCALE + bias[t]
            parts = []
            for h in range(heads):
                s = scores[:, h * PAIR:(h + 1) * PAIR]
                e = jnp.exp(s - jnp.max(s, -1, keepdims=True))
                parts.append(e * (1.0 / jnp.sum(e, -1, keepdims=True)))
            probs = jnp.concatenate(parts, axis=1)
            if backward:
                probs_s[t] = probs
            att_s[rows, lanes(0)] = mm(
                probs.astype(jnp.bfloat16), spread(qkv_s[rows, lanes(2)])
            ).astype(jnp.bfloat16)
            return c

        lax.fori_loop(0, steps, attend, 0)
        middle = x_s[...] + (mm(att_s[...], wproj[...]) + vecs[2:3])
        x_s[...] = middle
        unit_two, inv_two = unit(middle)
        b_s[...] = (unit_two * vecs[3:4] + vecs[4:5]).astype(jnp.bfloat16)
        acc_s[...] = jnp.zeros_like(acc_s)
        if backward:
            u2_s[...] = unit_two
            dy_s[...] = mm(perm[...], cot_ref[i]).astype(jnp.bfloat16)
            db_s[...] = jnp.zeros_like(db_s)

        def ffn(c, k):
            cols = pl.ds(pl.multiple_of(c * CHUNK, CHUNK), CHUNK)
            hidden = mm(b_s[...], w1[:, cols]) + b1[:, cols]
            cdf = 0.5 * (1.0 + lax.erf(hidden * (1.0 / math.sqrt(2.0))))
            act = (hidden * cdf).astype(jnp.bfloat16)
            acc_s[...] += mm(act, w2[cols, :])
            if backward:
                pdf = jnp.exp(-0.5 * hidden * hidden) * (1.0 / math.sqrt(2.0 * math.pi))
                dact = mm_t(dy_s[...], w2[cols, :])
                dhid_f = dact * (cdf + hidden * pdf)
                dhid = dhid_f.astype(jnp.bfloat16)
                g2[cols, :] += mm_outer(act, dy_s[...])
                g1[:, cols] += mm_outer(b_s[...], dhid)
                gfc1b[:, cols] += col(dhid.astype(jnp.float32))
                db_s[...] += mm_t(dhid, w1[:, cols])
            return k

        lax.fori_loop(0, w1.shape[1] // CHUNK, ffn, 0)
        out = (x_s[...] + (acc_s[...] + vecs[5:6])).astype(jnp.bfloat16)
        out_ref[i] = mm(back[...], out).astype(jnp.bfloat16)
        if not backward:
            return carry
        db = db_s[...]
        gvec[3:4] += col(db * u2_s[...])
        gvec[4:5] += col(db)
        dy = dy_s[...].astype(jnp.float32)
        gvec[5:6] += col(dy)
        dmid = dy + unit_back(db, u2_s[...], inv_two, vecs[3:4])
        x_s[...] = dmid
        dz = dmid.astype(jnp.bfloat16)
        gvec[2:3] += col(dz.astype(jnp.float32))
        gproj[...] += mm_outer(att_s[...], dz)
        datt_s[...] = mm_t(dz, wproj[...]).astype(jnp.bfloat16)

        def attend_back(t, c):
            rows, g, lanes = place(t)
            datt = datt_s[rows, lanes(0)]
            probs = probs_s[t]
            dprobs = mm_t(datt, spread(qkv_s[rows, lanes(2)]))
            dqkv_s[rows, lanes(2)] = gathered(
                mm_outer(probs.astype(jnp.bfloat16), datt)
            ).astype(jnp.bfloat16)
            parts = []
            for h in range(heads):
                here = slice(h * PAIR, (h + 1) * PAIR)
                p = probs[:, here]
                d = dprobs[:, here]
                parts.append(p * (d - jnp.sum(p * d, -1, keepdims=True)))
            dscores = jnp.concatenate(parts, axis=1).astype(jnp.bfloat16)
            drel[g] += dscores.astype(jnp.float32)
            dqkv_s[rows, lanes(0)] = (
                mm(dscores, spread(qkv_s[rows, lanes(1)])) * SCALE
            ).astype(jnp.bfloat16)
            dqkv_s[rows, lanes(1)] = (
                gathered(mm_outer(dscores, qkv_s[rows, lanes(0)])) * SCALE
            ).astype(jnp.bfloat16)
            return c

        lax.fori_loop(0, steps, attend_back, 0)
        for part in range(3):
            cols = slice(part * channels, (part + 1) * channels)
            gqkv[:, cols] += mm_outer(a_s[...], dqkv_s[:, cols])
            gcol[:, cols] += col(dqkv_s[:, cols].astype(jnp.float32))
        da = mm_t(dqkv_s[...], wqkv[...])
        gvec[0:1] += col(da * u1_s[...])
        gvec[1:2] += col(da)
        dx = x_s[...] + unit_back(da, u1_s[...], inv_one, vecs[0:1])
        high = dx.astype(jnp.bfloat16)
        rest = (dx - high.astype(jnp.float32)).astype(jnp.bfloat16)
        dx_ref[i] = mm(back[...], high) + mm(back[...], rest)
        return carry

    lax.fori_loop(0, x_ref.shape[0], one_image, 0)
    if backward:
        gqkv_o[...] = gqkv[...].astype(jnp.bfloat16)
        gproj_o[...] = gproj[...].astype(jnp.bfloat16)
        g1_o[...] = g1[...].astype(jnp.bfloat16)
        g2_o[...] = g2[...].astype(jnp.bfloat16)


def call_layer(x, cot, consts, mats, small):
    perm, back, hm = consts
    wqkv, wproj, w1, w2 = mats
    bqkv, vecs, b1, bias = small
    backward = cot is not None
    n = x.shape[0]
    c, f = w1.shape
    low, full = jnp.bfloat16, jnp.float32
    t = bias.shape[0]
    tokens = (ROWS, c)
    heads = PAIR // HEAD
    outs = [jax.ShapeDtypeStruct((n,) + tokens, low)]
    scratch = [
        pltpu.VMEM(tokens, full),
        pltpu.VMEM(tokens, low),
        pltpu.VMEM((ROWS, 3 * c), low),
        pltpu.VMEM(tokens, low),
        pltpu.VMEM(tokens, low),
        pltpu.VMEM(tokens, full),
    ]
    if backward:
        outs += [
            jax.ShapeDtypeStruct((n,) + tokens, full),
            jax.ShapeDtypeStruct(wqkv.shape, low),
            jax.ShapeDtypeStruct(wproj.shape, low),
            jax.ShapeDtypeStruct(w1.shape, low),
            jax.ShapeDtypeStruct(w2.shape, low),
            jax.ShapeDtypeStruct((8, c), full),
            jax.ShapeDtypeStruct((1, 3 * c), full),
            jax.ShapeDtypeStruct((1, f), full),
            jax.ShapeDtypeStruct((c // PAIR, PAIR, heads * PAIR), full),
        ]
        scratch += [
            pltpu.VMEM((t, PAIR, heads * PAIR), full),
            pltpu.VMEM(tokens, full),
            pltpu.VMEM(tokens, full),
            pltpu.VMEM(tokens, low),
            pltpu.VMEM(tokens, full),
            pltpu.VMEM((ROWS, 3 * c), low),
            pltpu.VMEM(tokens, low),
            pltpu.VMEM(wqkv.shape, full),
            pltpu.VMEM(wproj.shape, full),
            pltpu.VMEM(w1.shape, full),
            pltpu.VMEM(w2.shape, full),
        ]
    args = (x,) + ((cot,) if backward else ())
    args += (perm, back, wqkv, bqkv, wproj, vecs, w1, b1, w2, bias, hm)
    vmem = pl.BlockSpec(memory_space=pltpu.VMEM)
    return pl.pallas_call(
        functools.partial(layer_kernel, backward),
        out_shape=outs,
        in_specs=[vmem] * len(args),
        out_specs=[vmem] * len(outs),
        scratch_shapes=scratch,
        compiler_params=pltpu.CompilerParams(vmem_limit_bytes=58 * 2**20),
        cost_estimate=pl.CostEstimate(
            flops=2 * n * ROWS * c * (4 * c + 2 * f) * (3 if backward else 1),
            bytes_accessed=2 * c * (4 * c + 2 * f),
            transcendentals=n * ROWS * f,
        ),
    )(*args)


def window_order(offset):
    matrix = np.zeros((ROWS, ROWS), np.float32)
    side = GRID // WIN
    for w in range(side * side):
        for i in range(WIN * WIN):
            row = (w // side) * WIN + i // WIN
            column = (w % side) * WIN + i % WIN
            token = ((row + offset) % GRID) * GRID + (column + offset) % GRID
            matrix[w * SLOT + i, token] = 1.0
    return matrix


def window_bias(rel, mask):
    heads = rel.shape[0]
    count = mask.shape[0]
    area = WIN * WIN
    more = SLOT - area
    block = rel[None] + mask[:, None]
    block = jnp.pad(block, ((0, 0), (0, 0), (0, more), (0, 0)))
    block = jnp.pad(block, ((0, 0), (0, 0), (0, 0), (0, more)), constant_values=FAR)
    block = block.reshape(count // 2, 2, heads, SLOT, SLOT)
    first = jnp.pad(block[:, 0], ((0, 0), (0, 0), (0, 0), (0, SLOT)), constant_values=FAR)
    second = jnp.pad(block[:, 1], ((0, 0), (0, 0), (0, 0), (SLOT, 0)), constant_values=FAR)
    both = jnp.concatenate([first, second], axis=2)
    per = PAIR // HEAD
    both = both.reshape(count // 2, heads // per, per, PAIR, PAIR).transpose(0, 1, 3, 2, 4)
    return both.reshape(count // 2 * (heads // per), PAIR, per * PAIR)


def table_grad(drel, onehot):
    groups = drel.shape[0]
    area = WIN * WIN
    split = drel.reshape(groups, 2, SLOT, PAIR // HEAD, 2, SLOT)
    total = split[:, 0, :area, :, 0, :area] + split[:, 1, :area, :, 1, :area]
    return jnp.einsum("ijr,gihj->rgh", onehot, total, precision=lax.Precision.HIGHEST).reshape(
        onehot.shape[-1], -1
    )


def to_windows(tensor):
    side = GRID // WIN
    lattice = tensor.reshape(side, WIN, side, WIN).transpose(0, 2, 1, 3)
    return lattice.reshape(side * side, WIN * WIN)


def shards(
    images,
    cotangent,
    region,
    rel_index,
    norm1_gain,
    norm1_bias,
    w_qkv,
    qv_bias,
    rel_table,
    w_proj,
    proj_bias,
    norm2_gain,
    norm2_bias,
    w_fc1,
    fc1_bias,
    w_fc2,
    fc2_bias,
):
    section_id = lax.axis_index("section")
    first = section_id == 0
    micro, per, tokens, channels = images.shape
    half = micro // 2
    table_rows = rel_table.shape[1]
    heads = rel_table.shape[2]
    hidden = fc1_bias.shape[1]

    def quarter(part):
        rows = part.shape[0] // lax.axis_size("rep")
        return lax.dynamic_slice_in_dim(part, lax.axis_index("rep") * rows, rows, 0)

    own_mats = tuple(
        lax.all_gather(quarter(part[0]), ("shard", "rep"), axis=0, tiled=True)
        for part in (w_qkv, w_proj, w_fc1, w_fc2)
    )
    from_zero = [(0, 1)]
    from_one = [(1, 0)]

    def moved(tree, route):
        return jax.tree.map(lambda part: lax.ppermute(part, "section", route), tree)

    def choose(on_zero, on_one):
        return jax.tree.map(lambda l, r: jnp.where(first, l, r), on_zero, on_one)

    mats_zero = choose(own_mats, moved(own_mats, from_zero))
    mats_one = choose(moved(own_mats, from_one), own_mats)
    small_list = (
        norm1_gain, norm1_bias, proj_bias, norm2_gain, norm2_bias, fc2_bias, qv_bias, fc1_bias,
        rel_table,
    )
    small_flat = jnp.concatenate([part.reshape(-1) for part in small_list])
    small_both = lax.all_gather(small_flat, "section", axis=0)
    onehot = (
        rel_index[:, :, None] == jnp.arange(table_rows, dtype=jnp.int32)[None, None, :]
    ).astype(jnp.float32)
    labels = to_windows(region)
    region_mask = jnp.where(labels[:, :, None] == labels[:, None, :], 0.0, -100.0).astype(
        jnp.float32
    )

    def small_of(layer):
        flat = small_both[layer]
        six = flat[: 6 * channels].reshape(6, channels)
        vecs = jnp.pad(six, ((0, 2), (0, 0)))
        at = 6 * channels
        qv = flat[at:at + 2 * channels]
        at += 2 * channels
        b1 = flat[at:at + hidden]
        at += hidden
        table = flat[at:].reshape(table_rows, heads)
        bqkv = jnp.concatenate([qv[:channels], jnp.zeros((channels,), jnp.float32), qv[channels:]])
        rel = jnp.einsum("ijr,rh->hij", onehot, table, precision=lax.Precision.HIGHEST)
        mask = region_mask if layer == 1 else jnp.zeros_like(region_mask)
        return (bqkv[None], vecs, b1[None], window_bias(rel, mask))

    lane_head = np.arange(PAIR) // HEAD
    hm = np.zeros((PAIR // HEAD, PAIR, PAIR), np.float32)
    for h in range(PAIR // HEAD):
        hm[h] = lane_head == h
    hm = jnp.asarray(hm.reshape(-1, PAIR), jnp.bfloat16)

    def consts_of(offset):
        perm = window_order(offset)
        return jnp.asarray(perm, jnp.bfloat16), jnp.asarray(perm.T, jnp.bfloat16), hm

    def mine(array):
        part = lax.dynamic_slice_in_dim(array, section_id * half, half, 0)
        part = part.reshape(half * per, tokens, channels)
        return jnp.pad(part, ((0, 0), (0, ROWS - tokens), (0, 0)))

    def trimmed(array):
        return array[:, :tokens].reshape(half, per, tokens, channels)

    x0 = mine(images)
    cot = mine(cotangent)
    consts_zero, consts_one = consts_of(0), consts_of(SHIFT)
    small_zero, small_one = small_of(0), small_of(1)
    (x1,) = call_layer(x0, None, consts_zero, mats_zero, small_zero)
    res_one = call_layer(x1, cot, consts_one, mats_one, small_one)
    out_one, dx_one, big_one = res_one[0], res_one[1], tuple(res_one[2:6])
    sent_one = moved((trimmed(out_one), trimmed(dx_one), big_one), from_zero)
    res_zero = call_layer(x0, dx_one.astype(jnp.bfloat16), consts_zero, mats_zero, small_zero)
    dx_zero, big_zero = res_zero[1], tuple(res_zero[2:6])
    x1_there = moved(trimmed(x1), from_one)
    dx_there, big_there = moved((trimmed(dx_zero), big_zero), from_one)

    def whole(zero_own, zero_there, one_own, one_there):
        on_zero = jnp.concatenate([zero_own, zero_there], 0)
        on_one = jnp.concatenate([one_there, one_own], 0)
        return jnp.where(first, on_zero, on_one)[None]

    section_out = whole(trimmed(x1), x1_there, trimmed(out_one), sent_one[0])
    input_grad = whole(trimmed(dx_zero), dx_there, trimmed(dx_one), sent_one[1])

    def summed(zero_own, zero_there, one_own, one_there):
        own = jnp.where(first, zero_own, one_own).astype(jnp.float32)
        there = jnp.where(first, zero_there, one_there).astype(jnp.float32)
        return (own + there).astype(jnp.bfloat16)

    big_total = jax.tree.map(summed, big_zero, big_there, big_one, sent_one[2])
    n_shard, n_rep = lax.axis_size("shard"), lax.axis_size("rep")

    def rep_major(part):
        split = part.reshape(n_shard, n_rep, -1, part.shape[1]).transpose(1, 0, 2, 3)
        return split.reshape(part.shape)

    big_total = jax.tree.map(rep_major, big_total)
    over_rep = lax.psum_scatter(big_total, "rep", scatter_dimension=0, tiled=True)
    owned = lax.psum_scatter(over_rep, "shard", scatter_dimension=0, tiled=True)
    rows_qkv, rows_proj, rows_fc1, rows_fc2 = jax.tree.map(
        lambda part: part.astype(jnp.float32), lax.all_gather(owned, "rep", axis=0, tiled=True)
    )

    def small_grads(res):
        gvec, gcol, gfc1b, drel = res[6:10]
        return jnp.concatenate(
            [
                gvec[:6].reshape(-1), gcol[0, :channels], gcol[0, 2 * channels:], gfc1b[0],
                table_grad(drel, onehot).reshape(-1),
            ]
        )

    small_sum = lax.psum(
        jnp.stack([small_grads(res_zero), small_grads(res_one)]), ("section", "shard", "rep")
    )
    flat = jnp.where(first, small_sum[0], small_sum[1])
    six = flat[: 6 * channels].reshape(6, 1, channels)
    at = 6 * channels
    qv_sum = flat[at:at + 2 * channels][None]
    at += 2 * channels
    fc1_sum = flat[at:at + hidden][None]
    table_sum = flat[at + hidden:].reshape(1, table_rows, heads)
    return (
        section_out,
        input_grad,
        six[0],
        six[1],
        rows_qkv[None],
        qv_sum,
        table_sum,
        rows_proj[None],
        six[2],
        six[3],
        six[4],
        rows_fc1[None],
        fc1_sum,
        rows_fc2[None],
        six[5],
    )


def solution(mesh):
    placed = (
        P(None, ("shard", "rep"), None, None),
        P(None, ("shard", "rep"), None, None),
        P(),
        P(),
        P("section", None),
        P("section", None),
        P("section", "shard", None),
        P("section", None),
        P("section", None, None),
        P("section", "shard", None),
        P("section", None),
        P("section", None),
        P("section", None),
        P("section", "shard", None),
        P("section", None),
        P("section", "shard", None),
        P("section", None),
    )
    return jax.shard_map(
        shards,
        mesh=mesh,
        in_specs=placed,
        out_specs=(
            P("section", None, ("shard", "rep"), None, None),
            P("section", None, ("shard", "rep"), None, None),
            P("section", None),
            P("section", None),
            P("section", "shard", None),
            P("section", None),
            P("section", None, None),
            P("section", "shard", None),
            P("section", None),
            P("section", None),
            P("section", None),
            P("section", "shard", None),
            P("section", None),
            P("section", "shard", None),
            P("section", None),
        ),
        check_vma=False,
    )
```
